32 devices in a mesh: row: 8 (over z, x), col: 4 (over y, core).
Axes of the slice: x: 2, y: 2, z: 4, core: 2. Of those that a mesh axis runs over, the one named last changes fastest.
Arguments:
- traces: bfloat16 [4096, 1024], P(('row', 'col'))
- alive: int32 [4096], P(('row', 'col')), may hold values 0 or 1
- pair_list: int32 [128, 2], P(('row', 'col')), may hold values from -1 to 31, as said below
Outputs:
- correlations: bfloat16 [128, 128, 65, 128], P(('row', 'col'))
The draws below stay inside these ranges and needn't reach their ends.
Inputs may be any that keep to these rules, and one draw needn't show every extreme that they name: `pair_list`: slots p * 4 to (p + 1) * 4 - 1 belong to flat device p = r * 4 + c (r its row index, c its col index); they hold 1 to 4 live pairs first and then (-1, -1) pairs; in every draw some device has all 4 slots live. A live pair (a, b) of that device has a // 4 == r, b % 4 == c and b >= a.
All inputs are finite; a program needn't handle non-finite values. No bound on the sum of `alive` on one device may be relied on, other than what follows from the above.
Results may differ from the reference program's by a relative error of at most 0.0042.
Values may be sent and summed in bfloat16 or wider, within the bound.
A program may use at most 128 MiB of HBM per device.

```python
import jax
import jax.numpy as jnp
from jax import lax

BLK = 128
LAGS = 65
SAMPLES = 1024
SLOTS = 4
CHANNELS = 4096
N_ROW = 8
N_COL = 4
DEVICES = 32


def draw_traces(key, part):
    keys = jax.random.split(key, 4)
    delays = jax.random.randint(keys[0], (CHANNELS,), 0, (LAGS - 1) // 2)
    source = jax.random.normal(keys[1], (SAMPLES + LAGS,), jnp.float32)
    positions = jnp.arange(SAMPLES)[None, :] + delays[:, None]
    coherent = jnp.take(source, positions)
    amplitude = jnp.exp(jax.random.uniform(keys[3], (CHANNELS, 1), jnp.float32, -1.5, 1.5))
    noise = jax.random.normal(keys[2], (CHANNELS, SAMPLES), jnp.float32)
    mixed = 0.8 * coherent + 0.6 * noise
    return (amplitude * mixed).astype(jnp.bfloat16)


def draw_pair_list(key, part):
    keys = jax.random.split(key, 4)
    device = jnp.arange(DEVICES, dtype=jnp.int32)
    counts = jax.random.randint(keys[0], (DEVICES,), 1, SLOTS + 1)
    fullest = jax.random.randint(keys[1], (), 0, DEVICES)
    counts = jnp.where((device == fullest) | (device == 0), SLOTS, counts)
    row_index = jnp.broadcast_to((device // N_COL)[:, None], (DEVICES, SLOTS))
    col_index = jnp.broadcast_to((device % N_COL)[:, None], (DEVICES, SLOTS))
    target = row_index + jax.random.randint(keys[2], (DEVICES, SLOTS), 0, 1048576) % (N_ROW - row_index)
    slot_index = jnp.broadcast_to(jnp.arange(SLOTS, dtype=jnp.int32)[None, :], (DEVICES, SLOTS))
    forced = jnp.where(slot_index == 0, N_ROW - 1, jnp.where(slot_index == 1, N_ROW // 2, target))
    target = jnp.where(device[:, None] == 0, forced, target)
    highest = jnp.where(target == row_index, col_index + 1, N_COL)
    picked = jax.random.randint(keys[3], (DEVICES, SLOTS), 0, 1048576) % highest
    first = row_index * N_COL + picked
    second = target * N_COL + col_index
    living = slot_index < counts[:, None]
    first = jnp.where(living, first, -1)
    second = jnp.where(living, second, -1)
    return jnp.stack([first, second], axis=-1).reshape(DEVICES * SLOTS, 2).astype(jnp.int32)


def place_ends(array, rng, low, high):
    longest = array.shape.index(max(array.shape))
    spots = []
    for shift in (0, 1):
        where = [jax.random.randint(jax.random.fold_in(rng, axis), (), 0, length) for axis, length in enumerate(array.shape)]
        where[longest] = (where[longest] + shift) % array.shape[longest]
        spots.append(tuple(where))
    return array.at[spots[0]].set(low).at[spots[1]].set(high)


def setup_inputs(seed: int = 0) -> dict:
    key_list = jax.random.split(jax.random.key(seed), 4)
    traces = draw_traces(jax.random.fold_in(key_list[3], 71), 0)
    alive = place_ends((jax.random.randint(key_list[1], (CHANNELS,), 0, 10) < 9).astype(jnp.int32), jax.random.fold_in(key_list[1], 1), 0, 1)
    pair_list = draw_pair_list(jax.random.fold_in(key_list[3], 71), 0)
    return {"traces": traces, "alive": alive, "pair_list": pair_list}


def whiten(traces, alive):
    samples = traces.astype(jnp.float32)
    centered = samples - lax.optimization_barrier(jnp.mean(samples, axis=1, keepdims=True))
    power = lax.optimization_barrier(jnp.mean(centered * centered, axis=1, keepdims=True))
    factor = alive.astype(jnp.float32)[:, None] / jnp.sqrt(power + 1e-05)
    return (centered * factor).astype(jnp.bfloat16)

def correlate(left_block, right_block):
    length = left_block.shape[1]
    width = left_block.shape[0]
    reach = (LAGS - 1) // 2
    padded = jnp.pad(right_block, ((0, 0), (reach, reach)))
    shifted = jnp.stack([padded[:, offset:offset + length] for offset in range(LAGS)], axis=0)
    shifted = shifted.reshape(LAGS * width, length)
    summed = lax.dot_general(left_block, shifted, (((1,), (1,)), ((), ())), preferred_element_type=jnp.float32)
    return (summed * (1.0 / length)).reshape(width, LAGS, width).astype(jnp.bfloat16)

def reference(traces, alive, pair_list):
    whitened = lax.optimization_barrier(whiten(traces, alive)).astype(jnp.float32)

    def one_pair(pair):
        first = pair[0]
        second = pair[1]

        def compute(unused):
            left_block = lax.dynamic_slice_in_dim(whitened, (jnp.maximum(first, 0) * BLK).astype(jnp.int32), BLK, 0)
            right_block = lax.dynamic_slice_in_dim(whitened, (jnp.maximum(second, 0) * BLK).astype(jnp.int32), BLK, 0)
            return correlate(left_block, right_block)

        def empty(unused):
            return jnp.zeros((BLK, LAGS, BLK), jnp.bfloat16)
        return lax.cond(first >= 0, compute, empty, 0)
    return lax.map(one_pair, pair_list)
```

```python
import functools

import jax
import jax.numpy as jnp
from jax import lax
from jax.experimental import pallas as pl
from jax.experimental.pallas import tpu as pltpu
from jax.sharding import PartitionSpec as P

LAGS = 65
REACH = (LAGS - 1) // 2
STEP = 8
MESH = pl.DeviceIdType.MESH


def whiten(traces, alive):
    samples = traces.astype(jnp.float32)
    centered = samples - jnp.mean(samples, axis=1, keepdims=True)
    power = jnp.mean(centered * centered, axis=1, keepdims=True)
    factor = alive.astype(jnp.float32) / jnp.sqrt(power + 1e-05)
    return (centered * factor).astype(jnp.bfloat16)


def gather_kernel(grid, traces_ref, alive_ref, row_ref, col_ref, own, z_send, x_send, y_send,
                  col_recv, row_recv, local_sem):
    deep, wide, across = grid
    row, col = lax.axis_index("row"), lax.axis_index("col")
    z, x = row // wide, row % wide

    def at(r, c):
        return (r, c)

    barrier = pltpu.get_barrier_semaphore()

    def greet(r, c):
        pl.semaphore_signal(barrier, inc=1, device_id=at(r, c), device_id_type=MESH)

    pl.when(z > 0)(lambda: greet(row - wide, col))
    pl.when(z < deep - 1)(lambda: greet(row + wide, col))
    for step in range(1, wide):
        greet(z * wide + (x + step) % wide, col)
    for step in range(1, across):
        greet(row, (col + step) % across)

    alive = jnp.broadcast_to(alive_ref[...].astype(jnp.float32), (own.shape[0], own.shape[0]))
    own[...] = whiten(traces_ref[...], alive.T[:, :1])

    peers = wide - 1 + across - 1 + (z > 0).astype(jnp.int32) + (z < deep - 1).astype(jnp.int32)
    pl.semaphore_wait(barrier, peers)

    def down(source, block):
        return pltpu.make_async_remote_copy(
            src_ref=source, dst_ref=col_ref.at[block], send_sem=z_send.at[block // wide],
            recv_sem=col_recv.at[block], device_id=at(row - wide, col), device_id_type=MESH)

    def side(source, block, step):
        return pltpu.make_async_remote_copy(
            src_ref=source, dst_ref=col_ref.at[block], send_sem=x_send.at[block // wide, step],
            recv_sem=col_recv.at[block], device_id=at(z * wide + (x + step) % wide, col),
            device_id_type=MESH)

    def along(step):
        return pltpu.make_async_remote_copy(
            src_ref=own, dst_ref=row_ref.at[col], send_sem=y_send.at[step],
            recv_sem=row_recv.at[col], device_id=at(row, (col + step) % across),
            device_id_type=MESH)

    def arrived(ref, place, sem):
        pltpu.make_async_copy(ref.at[place], ref.at[place], sem.at[place]).wait()

    pl.when(z > 0)(lambda: down(own, row).start())
    for step in range(1, wide):
        pl.when((x + step) % wide < x)(lambda step=step: side(own, row, step).start())
    for step in range(1, across):
        along(step).start()
    keep_col = pltpu.make_async_copy(own, col_ref.at[row], local_sem.at[0])
    keep_row = pltpu.make_async_copy(own, row_ref.at[col], local_sem.at[1])
    keep_col.start()
    keep_row.start()

    for hop in range(1, deep):
        @pl.when(z + hop < deep)
        def _(hop=hop):
            block = row + hop * wide
            arrived(col_ref, block, col_recv)
            pl.when(z > 0)(lambda: down(col_ref.at[block], block).start())
            for step in range(1, wide):
                side(col_ref.at[block], block, step).start()

    for step in range(1, wide):
        other = (x + step) % wide
        pl.when(other > x)(lambda other=other: arrived(col_ref, z * wide + other, col_recv))
        for hop in range(1, deep):
            pl.when(z + hop < deep)(
                lambda other=other, hop=hop: arrived(col_ref, (z + hop) * wide + other, col_recv))
    for step in range(1, across):
        arrived(row_ref, (col + step) % across, row_recv)

    keep_col.wait()
    keep_row.wait()
    pl.when(z > 0)(lambda: down(own, row).wait_send())
    for step in range(1, wide):
        pl.when((x + step) % wide < x)(lambda step=step: side(own, row, step).wait_send())
    for step in range(1, across):
        along(step).wait_send()
    for hop in range(1, deep):
        @pl.when(z + hop < deep)
        def _(hop=hop):
            block = row + hop * wide
            pl.when(z > 0)(lambda: down(col_ref.at[block], block).wait_send())
            for step in range(1, wide):
                side(col_ref.at[block], block, step).wait_send()


def gather(traces, alive):
    block, length = traces.shape
    rows, across = lax.axis_size("row"), lax.axis_size("col")
    deep = 4 if rows % 4 == 0 else 1
    wide = rows // deep
    return pl.pallas_call(
        functools.partial(gather_kernel, (deep, wide, across)),
        out_shape=(
            jax.ShapeDtypeStruct((across, block, length), jnp.bfloat16),
            jax.ShapeDtypeStruct((rows, block, length), jnp.bfloat16),
        ),
        in_specs=[pl.BlockSpec(memory_space=pltpu.VMEM)] * 2,
        out_specs=(pl.BlockSpec(memory_space=pl.ANY), pl.BlockSpec(memory_space=pl.ANY)),
        scratch_shapes=[
            pltpu.VMEM((block, length), jnp.bfloat16),
            pltpu.SemaphoreType.DMA((deep,)),
            pltpu.SemaphoreType.DMA((deep, wide)),
            pltpu.SemaphoreType.DMA((across,)),
            pltpu.SemaphoreType.DMA((rows,)),
            pltpu.SemaphoreType.DMA((across,)),
            pltpu.SemaphoreType.DMA((2,)),
        ],
        compiler_params=pltpu.CompilerParams(
            collective_id=0, has_side_effects=True, vmem_limit_bytes=32 * 1024 * 1024),
        name="gather",
    )(traces, alive.reshape(1, block))


def shifted(array, amount):
    width, length = array.shape
    if amount == 0:
        return array
    empty = jnp.zeros((width, abs(amount)), array.dtype)
    if amount > 0:
        return jnp.concatenate([empty, array[:, : length - amount]], axis=1)
    return jnp.concatenate([array[:, -amount:], empty], axis=1)


def pair_kernel(row_place, col_place, live, left_ref, right_ref, out_ref, lefts, rights):
    slot = pl.program_id(0)
    width, length = left_ref.shape[1:]
    scale = 1.0 / length

    def product(a, b):
        return lax.dot_general(
            a, b, (((1,), (1,)), ((), ())), preferred_element_type=jnp.float32)

    @pl.when(live[slot] == 0)
    def _():
        out_ref[...] = jnp.zeros_like(out_ref)

    @pl.when(live[slot] != 0)
    def _():
        left, right = left_ref[0], right_ref[0]
        out_ref[0, REACH] = (product(left, right) * scale).astype(jnp.bfloat16)
        for sign in (1, -1):
            for shift in range(STEP):
                lefts[shift * width : (shift + 1) * width, :] = shifted(left, sign * (shift + 1))
            for pair in range(REACH // STEP // 2):
                for half in range(2):
                    rights[half * width : (half + 1) * width, :] = shifted(
                        right, -sign * STEP * (2 * pair + half))
                summed = product(lefts[...], rights[...])
                scaled = (summed * scale).astype(jnp.bfloat16)
                for half in range(2):
                    for shift in range(STEP):
                        lag = REACH + sign * (STEP * (2 * pair + half) + shift + 1)
                        out_ref[0, lag] = scaled[
                            shift * width : (shift + 1) * width, half * width : (half + 1) * width]


def correlate(row_place, col_place, live, row_panel, col_panel):
    slots = live.shape[0]
    _, width, length = row_panel.shape
    return pl.pallas_call(
        pair_kernel,
        grid_spec=pltpu.PrefetchScalarGridSpec(
            num_scalar_prefetch=3,
            grid=(slots,),
            in_specs=[
                pl.BlockSpec((1, width, length), lambda s, r, c, l: (r[s], 0, 0)),
                pl.BlockSpec((1, width, length), lambda s, r, c, l: (c[s], 0, 0)),
            ],
            out_specs=pl.BlockSpec((1, LAGS, width, width), lambda s, r, c, l: (s, 0, 0, 0)),
            scratch_shapes=[
                pltpu.VMEM((STEP * width, length), jnp.bfloat16),
                pltpu.VMEM((2 * width, length), jnp.bfloat16),
            ],
        ),
        out_shape=jax.ShapeDtypeStruct((slots, LAGS, width, width), jnp.bfloat16),
        compiler_params=pltpu.CompilerParams(vmem_limit_bytes=48 * 1024 * 1024),
        name="pairs",
    )(row_place, col_place, live, row_panel, col_panel)


def shards(traces, alive, pair_list):
    across = lax.axis_size("col")
    row_first = lax.axis_index("row") * across
    row_place = jnp.clip(pair_list[:, 0] - row_first, 0, across - 1)
    col_place = jnp.maximum(pair_list[:, 1], 0) // across
    live = (pair_list[:, 0] >= 0).astype(jnp.int32)
    row_panel, col_panel = gather(traces, alive)
    lagged = correlate(row_place, col_place, live, row_panel, col_panel)
    return jnp.transpose(lagged, (0, 2, 1, 3))


def solution(mesh):
    in_specs = (P(("row", "col"), None), P(("row", "col")), P(("row", "col"), None))
    out_specs = P(("row", "col"), None, None, None)
    return jax.shard_map(shards, mesh=mesh, in_specs=in_specs, out_specs=out_specs, check_vma=False)
```

```python
import functools

import jax
import jax.numpy as jnp
from jax import lax
from jax.experimental import pallas as pl
from jax.experimental.pallas import tpu as pltpu
from jax.sharding import PartitionSpec as P

LAGS = 65
REACH = (LAGS - 1) // 2
STEP = 8
PARTS = 4
MESH = pl.DeviceIdType.MESH


def whiten(traces, alive):
    samples = traces.astype(jnp.float32)
    centered = samples - jnp.mean(samples, axis=1, keepdims=True)
    power = jnp.mean(centered * centered, axis=1, keepdims=True)
    factor = alive.astype(jnp.float32) / jnp.sqrt(power + 1e-05)
    return (centered * factor).astype(jnp.bfloat16)


def in_hbm(array):
    return pltpu.with_memory_space_constraint(array, pltpu.HBM)


def gather_kernel(grid, traces_hbm, alive_hbm, row_ref, col_ref, traces_ref, alive_ref, own,
                  z_send, x_send, y_send, relay_send, col_recv, row_recv, local_sem, load_sem):
    deep, wide, across, parts = grid
    row, col = lax.axis_index("row"), lax.axis_index("col")
    z, x = row // wide, row % wide
    part = own.shape[0] // parts
    relayed = parts // 2 if wide == 2 and deep > 1 else 0
    relays = (z == 1) & (x == 0)
    spared = (z == 0) & (x == 1)

    load_alive = pltpu.make_async_copy(alive_hbm, alive_ref, load_sem.at[parts])
    load_alive.start()

    def piece(h):
        return pl.ds(h * part, part)

    def load(h):
        return pltpu.make_async_copy(
            traces_hbm.at[piece(h)], traces_ref.at[piece(h)], load_sem.at[h])

    for h in range(parts):
        load(h).start()

    barrier = pltpu.get_barrier_semaphore()

    def greet(r, c):
        pl.semaphore_signal(barrier, inc=1, device_id=(r, c), device_id_type=MESH)

    pl.when(z > 0)(lambda: greet(row - wide, col))
    pl.when(z < deep - 1)(lambda: greet(row + wide, col))
    for step in range(1, wide):
        greet(z * wide + (x + step) % wide, col)
    for step in range(1, across):
        greet(row, (col + step) % across)

    def down(source, block, h, sem):
        return pltpu.make_async_remote_copy(
            src_ref=source.at[piece(h)], dst_ref=col_ref.at[block, piece(h)], send_sem=sem,
            recv_sem=col_recv.at[block, h], device_id=(row - wide, col), device_id_type=MESH)

    def side(source, block, step, h):
        return pltpu.make_async_remote_copy(
            src_ref=source.at[piece(h)], dst_ref=col_ref.at[block, piece(h)],
            send_sem=x_send.at[block // wide, step, h], recv_sem=col_recv.at[block, h],
            device_id=(z * wide + (x + step) % wide, col), device_id_type=MESH)

    def along(step, h):
        return pltpu.make_async_remote_copy(
            src_ref=own.at[piece(h)], dst_ref=row_ref.at[col, piece(h)],
            send_sem=y_send.at[step, h], recv_sem=row_recv.at[col, h],
            device_id=(row, (col + step) % across), device_id_type=MESH)

    def arrived(ref, place, h, sem):
        spot = ref.at[place, piece(h)]
        pltpu.make_async_copy(spot, spot, sem.at[place, h]).wait()

    def send_own(h, verb):
        pl.when(z > 0)(lambda: verb(down(own, row, h, z_send.at[z, h])))
        for step in range(1, wide):
            pl.when((x + step) % wide < x)(lambda step=step: verb(side(own, row, step, h)))
        for step in range(1, across):
            verb(along(step, h))

    def send_on(hop, h, verb):
        block = row + hop * wide
        pl.when(z > 0)(lambda: verb(down(col_ref.at[block], block, h, z_send.at[z + hop, h])))
        for step in range(1, wide):
            go = lambda step=step: verb(side(col_ref.at[block], block, step, h))
            if hop == 1 and h < relayed:
                pl.when(jnp.logical_not(spared))(go)
            else:
                go()

    def relay(h, verb):
        block = row + 1
        verb(down(col_ref.at[block], block, h, relay_send.at[h]))

    start = lambda copy: copy.start()
    sent = lambda copy: copy.wait_send()

    load_alive.wait()
    alive = jnp.broadcast_to(alive_ref[...].astype(jnp.float32), (own.shape[0], own.shape[0]))
    alive = alive.T[:, :1]
    for h in range(parts):
        load(h).wait()
        spot = slice(h * part, (h + 1) * part)
        own[spot, :] = whiten(traces_ref[spot, :], alive[spot])
        if h == 0:
            peers = (z > 0).astype(jnp.int32) + (z < deep - 1).astype(jnp.int32)
            pl.semaphore_wait(barrier, peers + (wide - 1 + across - 1))
        send_own(h, start)
    keep_col = pltpu.make_async_copy(own, col_ref.at[row], local_sem.at[0])
    keep_row = pltpu.make_async_copy(own, row_ref.at[col], local_sem.at[1])
    keep_col.start()
    keep_row.start()

    for hop in range(1, deep):
        for h in range(parts):
            @pl.when(z + hop < deep)
            def _(hop=hop, h=h):
                arrived(col_ref, row + hop * wide, h, col_recv)
                send_on(hop, h, start)
        if hop == 1:
            for h in range(relayed):
                @pl.when(relays)
                def _(h=h):
                    arrived(col_ref, row + 1, h, col_recv)
                    relay(h, start)

    for step in range(1, wide):
        other = (x + step) % wide
        for h in range(parts):
            due = other > x
            if h < relayed:
                due = due & jnp.logical_not(relays)
            pl.when(due)(
                lambda other=other, h=h: arrived(col_ref, z * wide + other, h, col_recv))
            for hop in range(1, deep):
                pl.when(z + hop < deep)(lambda other=other, hop=hop, h=h: arrived(
                    col_ref, (z + hop) * wide + other, h, col_recv))
    for step in range(1, across):
        for h in range(parts):
            arrived(row_ref, (col + step) % across, h, row_recv)

    keep_col.wait()
    keep_row.wait()
    for h in range(parts):
        send_own(h, sent)
        for hop in range(1, deep):
            pl.when(z + hop < deep)(lambda hop=hop, h=h: send_on(hop, h, sent))
    for h in range(relayed):
        pl.when(relays)(lambda h=h: relay(h, sent))


def gather(traces, alive):
    block, length = traces.shape
    rows, across = lax.axis_size("row"), lax.axis_size("col")
    deep = 4 if rows % 4 == 0 else 1
    wide = rows // deep
    parts = PARTS
    return pl.pallas_call(
        functools.partial(gather_kernel, (deep, wide, across, parts)),
        out_shape=(
            jax.ShapeDtypeStruct((across, block, length), jnp.bfloat16),
            jax.ShapeDtypeStruct((rows, block, length), jnp.bfloat16),
        ),
        in_specs=[pl.BlockSpec(memory_space=pltpu.HBM)] * 2,
        out_specs=(pl.BlockSpec(memory_space=pl.ANY), pl.BlockSpec(memory_space=pl.ANY)),
        scratch_shapes=[
            pltpu.VMEM((block, length), jnp.bfloat16),
            pltpu.VMEM((1, block), jnp.int32),
            pltpu.VMEM((block, length), jnp.bfloat16),
            pltpu.SemaphoreType.DMA((deep, parts)),
            pltpu.SemaphoreType.DMA((deep, wide, parts)),
            pltpu.SemaphoreType.DMA((across, parts)),
            pltpu.SemaphoreType.DMA((parts,)),
            pltpu.SemaphoreType.DMA((rows, parts)),
            pltpu.SemaphoreType.DMA((across, parts)),
            pltpu.SemaphoreType.DMA((2,)),
            pltpu.SemaphoreType.DMA((parts + 1,)),
        ],
        compiler_params=pltpu.CompilerParams(
            collective_id=0, has_side_effects=True, vmem_limit_bytes=16 * 1024 * 1024),
        name="gather",
    )(in_hbm(traces), in_hbm(alive.reshape(1, block)))


def shifted(array, amount):
    width, length = array.shape
    empty = jnp.zeros((width, abs(amount)), array.dtype)
    if amount == 0:
        return array
    if amount > 0:
        return jnp.concatenate([empty, array[:, : length - amount]], axis=1)
    return jnp.concatenate([array[:, -amount:], empty], axis=1)


def pair_kernel(pair_ref, row_ref, col_ref, out_hbm, out_ref, lefts, rights, sems):
    across, width, length = row_ref.shape
    slots = out_ref.shape[0]
    scale = 1.0 / length
    row_first = lax.axis_index("row") * across
    pieces = ((0, REACH), (REACH, LAGS))

    def product(a, b):
        return lax.dot_general(
            a, b, (((1,), (1,)), ((), ())), preferred_element_type=jnp.float32)

    def store(slot, piece):
        spot = pl.ds(pieces[piece][0], pieces[piece][1] - pieces[piece][0])
        return pltpu.make_async_copy(
            out_ref.at[slot, spot], out_hbm.at[slot, spot], sems.at[slot, piece])

    def one_slot(slot, carry):
        first, second = pair_ref[0, slot], pair_ref[1, slot]

        @pl.when(first < 0)
        def _():
            out_ref[slot] = jnp.zeros(out_ref.shape[1:], out_ref.dtype)
            store(slot, 0).start()
            store(slot, 1).start()

        @pl.when(first >= 0)
        def _():
            left = row_ref[jnp.clip(first - row_first, 0, across - 1)]
            right = col_ref[jnp.maximum(second, 0) // across]
            for side, sign in enumerate((-1, 1)):
                if sign == 1:
                    out_ref[slot, REACH] = (product(left, right) * scale).astype(jnp.bfloat16)
                for shift in range(STEP):
                    lefts[side, shift * width : (shift + 1) * width, :] = shifted(
                        left, sign * (shift + 1))
                for pair in range(REACH // STEP // 2):
                    for half in range(2):
                        rights[side, pair, half * width : (half + 1) * width, :] = shifted(
                            right, -sign * STEP * (2 * pair + half))
                    summed = product(lefts[side], rights[side, pair])
                    scaled = (summed * scale).astype(jnp.bfloat16)
                    for half in range(2):
                        for shift in range(STEP):
                            lag = REACH + sign * (STEP * (2 * pair + half) + shift + 1)
                            out_ref[slot, lag] = scaled[
                                shift * width : (shift + 1) * width,
                                half * width : (half + 1) * width]
                store(slot, side).start()

        return carry

    lax.fori_loop(0, slots, one_slot, 0)

    def finish(slot, carry):
        store(slot, 0).wait()
        store(slot, 1).wait()
        return carry

    lax.fori_loop(0, slots, finish, 0)


def correlate(pair_list, row_panel, col_panel):
    slots = pair_list.shape[0]
    _, width, length = row_panel.shape
    return pl.pallas_call(
        pair_kernel,
        in_specs=[
            pl.BlockSpec(memory_space=pltpu.SMEM),
            pl.BlockSpec(memory_space=pltpu.VMEM),
            pl.BlockSpec(memory_space=pltpu.VMEM),
        ],
        out_specs=pl.BlockSpec(memory_space=pltpu.HBM),
        out_shape=jax.ShapeDtypeStruct((slots, LAGS, width, width), jnp.bfloat16),
        scratch_shapes=[
            pltpu.VMEM((slots, LAGS, width, width), jnp.bfloat16),
            pltpu.VMEM((2, STEP * width, length), jnp.bfloat16),
            pltpu.VMEM((2, REACH // STEP // 2, 2 * width, length), jnp.bfloat16),
            pltpu.SemaphoreType.DMA((slots, 2)),
        ],
        compiler_params=pltpu.CompilerParams(vmem_limit_bytes=40 * 1024 * 1024),
        name="pairs",
    )(in_hbm(pair_list.T), row_panel, col_panel)


def shards(traces, alive, pair_list):
    row_panel, col_panel = gather(traces, alive)
    lagged = correlate(pair_list, row_panel, col_panel)
    return jnp.transpose(lagged, (0, 2, 1, 3))


def solution(mesh):
    in_specs = (P(("row", "col"), None), P(("row", "col")), P(("row", "col"), None))
    out_specs = P(("row", "col"), None, None, None)
    return jax.shard_map(shards, mesh=mesh, in_specs=in_specs, out_specs=out_specs, check_vma=False)
```

```python
import functools

import jax
import jax.numpy as jnp
from jax import lax
from jax.experimental import pallas as pl
from jax.experimental.pallas import tpu as pltpu
from jax.sharding import PartitionSpec as P

LAGS = 65
REACH = (LAGS - 1) // 2
STEP = 8
PARTS = 4
MESH = pl.DeviceIdType.MESH


def whiten(traces, alive):
    samples = traces.astype(jnp.float32)
    centered = samples - jnp.mean(samples, axis=1, keepdims=True)
    power = jnp.mean(centered * centered, axis=1, keepdims=True)
    factor = alive.astype(jnp.float32) / jnp.sqrt(power + 1e-05)
    return (centered * factor).astype(jnp.bfloat16)


def in_hbm(array):
    return pltpu.with_memory_space_constraint(array, pltpu.HBM)


def gather_kernel(grid, traces_hbm, alive_hbm, row_ref, col_ref, traces_ref, alive_ref, own,
                  z_send, x_send, y_send, relay_send, col_recv, row_recv, local_sem, load_sem):
    deep, wide, across, parts = grid
    row, col = lax.axis_index("row"), lax.axis_index("col")
    z, x = row // wide, row % wide
    part = own.shape[0] // parts
    relayed = parts // 2 if wide == 2 and deep > 1 else 0
    relays = (z == 1) & (x == 0)

    load_alive = pltpu.make_async_copy(alive_hbm, alive_ref, load_sem.at[parts])
    load_alive.start()

    def piece(h):
        return pl.ds(h * part, part)

    def load(h):
        return pltpu.make_async_copy(
            traces_hbm.at[piece(h)], traces_ref.at[piece(h)], load_sem.at[h])

    for h in range(parts):
        load(h).start()

    barrier = pltpu.get_barrier_semaphore()

    def greet(r, c):
        pl.semaphore_signal(barrier, inc=1, device_id=(r, c), device_id_type=MESH)

    pl.when(z > 0)(lambda: greet(row - wide, col))
    pl.when(z < deep - 1)(lambda: greet(row + wide, col))
    for step in range(1, wide):
        greet(z * wide + (x + step) % wide, col)
    for step in range(1, across):
        greet(row, (col + step) % across)

    def down(source, block, h, sem):
        return pltpu.make_async_remote_copy(
            src_ref=source.at[piece(h)], dst_ref=col_ref.at[block, piece(h)], send_sem=sem,
            recv_sem=col_recv.at[block, h], device_id=(row - wide, col), device_id_type=MESH)

    def side(source, block, step, h):
        return pltpu.make_async_remote_copy(
            src_ref=source.at[piece(h)], dst_ref=col_ref.at[block, piece(h)],
            send_sem=x_send.at[block // wide, step, h], recv_sem=col_recv.at[block, h],
            device_id=(z * wide + (x + step) % wide, col), device_id_type=MESH)

    def along(step, h):
        return pltpu.make_async_remote_copy(
            src_ref=own.at[piece(h)], dst_ref=row_ref.at[col, piece(h)],
            send_sem=y_send.at[step, h], recv_sem=row_recv.at[col, h],
            device_id=(row, (col + step) % across), device_id_type=MESH)

    def arrived(ref, place, h, sem):
        spot = ref.at[place, piece(h)]
        pltpu.make_async_copy(spot, spot, sem.at[place, h]).wait()

    def pass_down(hop, h, verb):
        block = row + hop * wide
        source = col_ref.at[block] if hop else own
        pl.when((z > 0) & (z + hop < deep))(
            lambda: verb(down(source, block, h, z_send.at[z + hop, h])))

    def pass_aside(hop, h, verb):
        block = row + hop * wide
        for step in range(1, wide):
            if hop == 0:
                due = (x + step) % wide < x
            elif hop == 1 and h < relayed:
                due = (z + hop < deep) & ((z != 0) | (x != 1))
            else:
                due = z + hop < deep
            source = col_ref.at[block] if hop else own
            pl.when(due)(lambda step=step: verb(side(source, block, step, h)))

    def pass_along(h, verb):
        for step in range(1, across):
            verb(along(step, h))

    def pass_on(hop, h):
        pass_down(hop, h, start)
        pass_aside(hop, h, start)

    def relay(h, verb):
        block = row + 1
        verb(down(col_ref.at[block], block, h, relay_send.at[h]))

    start = lambda copy: copy.start()
    sent = lambda copy: copy.wait_send()

    load_alive.wait()
    alive = jnp.broadcast_to(alive_ref[...].astype(jnp.float32), (own.shape[0], own.shape[0]))
    alive = alive.T[:, :1]
    for h in range(parts):
        load(h).wait()
        spot = slice(h * part, (h + 1) * part)
        own[spot, :] = whiten(traces_ref[spot, :], alive[spot])
        if h == 0:
            peers = (z > 0).astype(jnp.int32) + (z < deep - 1).astype(jnp.int32)
            pl.semaphore_wait(barrier, peers + (wide - 1 + across - 1))
        pass_on(0, h)
        pass_along(h, start)
    keep_col = pltpu.make_async_copy(own, col_ref.at[row], local_sem.at[0])
    keep_row = pltpu.make_async_copy(own, row_ref.at[col], local_sem.at[1])
    keep_col.start()
    keep_row.start()

    for hop in range(1, deep):
        for h in range(parts):
            pl.when(z + hop < deep)(
                lambda hop=hop, h=h: arrived(col_ref, row + hop * wide, h, col_recv))
            pass_on(hop, h)
    for h in range(relayed):
        @pl.when(relays)
        def _(h=h):
            arrived(col_ref, row + 1, h, col_recv)
            relay(h, start)

    for step in range(1, wide):
        other = (x + step) % wide
        for h in range(parts):
            due = other > x
            if h < relayed:
                due = due & jnp.logical_not(relays)
            pl.when(due)(
                lambda other=other, h=h: arrived(col_ref, z * wide + other, h, col_recv))
            for hop in range(1, deep):
                pl.when(z + hop < deep)(lambda other=other, hop=hop, h=h: arrived(
                    col_ref, (z + hop) * wide + other, h, col_recv))
    for step in range(1, across):
        for h in range(parts):
            arrived(row_ref, (col + step) % across, h, row_recv)

    keep_col.wait()
    keep_row.wait()
    for h in range(parts):
        pass_along(h, sent)
    for hop in range(deep):
        for h in range(parts):
            pass_down(hop, h, sent)
            pass_aside(hop, h, sent)
    for h in range(relayed):
        pl.when(relays)(lambda h=h: relay(h, sent))


def gather(traces, alive):
    block, length = traces.shape
    rows, across = lax.axis_size("row"), lax.axis_size("col")
    deep = 4 if rows % 4 == 0 else 1
    wide = rows // deep
    parts = PARTS
    return pl.pallas_call(
        functools.partial(gather_kernel, (deep, wide, across, parts)),
        out_shape=(
            jax.ShapeDtypeStruct((across, block, length), jnp.bfloat16),
            jax.ShapeDtypeStruct((rows, block, length), jnp.bfloat16),
        ),
        in_specs=[pl.BlockSpec(memory_space=pltpu.HBM)] * 2,
        out_specs=(pl.BlockSpec(memory_space=pl.ANY), pl.BlockSpec(memory_space=pl.ANY)),
        scratch_shapes=[
            pltpu.VMEM((block, length), jnp.bfloat16),
            pltpu.VMEM((1, block), jnp.int32),
            pltpu.VMEM((block, length), jnp.bfloat16),
            pltpu.SemaphoreType.DMA((deep, parts)),
            pltpu.SemaphoreType.DMA((deep, wide, parts)),
            pltpu.SemaphoreType.DMA((across, parts)),
            pltpu.SemaphoreType.DMA((parts,)),
            pltpu.SemaphoreType.DMA((rows, parts)),
            pltpu.SemaphoreType.DMA((across, parts)),
            pltpu.SemaphoreType.DMA((2,)),
            pltpu.SemaphoreType.DMA((parts + 1,)),
        ],
        compiler_params=pltpu.CompilerParams(
            collective_id=0, has_side_effects=True, vmem_limit_bytes=16 * 1024 * 1024),
        name="gather",
    )(in_hbm(traces), in_hbm(alive.reshape(1, block)))


def shifted(array, amount):
    width, length = array.shape
    empty = jnp.zeros((width, abs(amount)), array.dtype)
    if amount == 0:
        return array
    if amount > 0:
        return jnp.concatenate([empty, array[:, : length - amount]], axis=1)
    return jnp.concatenate([array[:, -amount:], empty], axis=1)


def pair_kernel(pair_ref, row_ref, col_ref, out_hbm, out_ref, lefts, rights, sems):
    across, width, length = row_ref.shape
    slots = out_ref.shape[0]
    scale = 1.0 / length
    row_first = lax.axis_index("row") * across
    pieces = ((0, REACH), (REACH, LAGS))

    def product(a, b):
        return lax.dot_general(
            a, b, (((1,), (1,)), ((), ())), preferred_element_type=jnp.float32)

    def store(slot, piece):
        spot = pl.ds(pieces[piece][0], pieces[piece][1] - pieces[piece][0])
        return pltpu.make_async_copy(
            out_ref.at[slot, spot], out_hbm.at[slot, spot], sems.at[slot, piece])

    def one_slot(slot, carry):
        first, second = pair_ref[0, slot], pair_ref[1, slot]

        @pl.when(first < 0)
        def _():
            out_ref[slot] = jnp.zeros(out_ref.shape[1:], out_ref.dtype)
            for piece in range(len(pieces)):
                store(slot, piece).start()

        @pl.when(first >= 0)
        def _():
            left = row_ref[jnp.clip(first - row_first, 0, across - 1)]
            right = col_ref[jnp.maximum(second, 0) // across]
            for side, sign in enumerate((-1, 1)):
                if sign == 1:
                    out_ref[slot, REACH] = (product(left, right) * scale).astype(jnp.bfloat16)
                for shift in range(STEP):
                    lefts[side, shift * width : (shift + 1) * width, :] = shifted(
                        left, sign * (shift + 1))
                for pair in range(REACH // STEP // 2):
                    for half in range(2):
                        rights[side, pair, half * width : (half + 1) * width, :] = shifted(
                            right, -sign * STEP * (2 * pair + half))
                    summed = product(lefts[side], rights[side, pair])
                    scaled = (summed * scale).astype(jnp.bfloat16)
                    for half in range(2):
                        for shift in range(STEP):
                            lag = REACH + sign * (STEP * (2 * pair + half) + shift + 1)
                            out_ref[slot, lag] = scaled[
                                shift * width : (shift + 1) * width,
                                half * width : (half + 1) * width]
                store(slot, side).start()

        return carry

    lax.fori_loop(0, slots, one_slot, 0)

    def finish(slot, carry):
        for piece in range(len(pieces)):
            store(slot, piece).wait()
        return carry

    lax.fori_loop(0, slots, finish, 0)


def correlate(pair_list, row_panel, col_panel):
    slots = pair_list.shape[0]
    _, width, length = row_panel.shape
    return pl.pallas_call(
        pair_kernel,
        in_specs=[
            pl.BlockSpec(memory_space=pltpu.SMEM),
            pl.BlockSpec(memory_space=pltpu.VMEM),
            pl.BlockSpec(memory_space=pltpu.VMEM),
        ],
        out_specs=pl.BlockSpec(memory_space=pltpu.HBM),
        out_shape=jax.ShapeDtypeStruct((slots, LAGS, width, width), jnp.bfloat16),
        scratch_shapes=[
            pltpu.VMEM((slots, LAGS, width, width), jnp.bfloat16),
            pltpu.VMEM((2, STEP * width, length), jnp.bfloat16),
            pltpu.VMEM((2, REACH // STEP // 2, 2 * width, length), jnp.bfloat16),
            pltpu.SemaphoreType.DMA((slots, 2)),
        ],
        compiler_params=pltpu.CompilerParams(vmem_limit_bytes=40 * 1024 * 1024),
        name="pairs",
    )(in_hbm(pair_list.T), row_panel, col_panel)


def shards(traces, alive, pair_list):
    row_panel, col_panel = gather(traces, alive)
    lagged = correlate(pair_list, row_panel, col_panel)
    return jnp.transpose(lagged, (0, 2, 1, 3))


def solution(mesh):
    in_specs = (P(("row", "col"), None), P(("row", "col")), P(("row", "col"), None))
    out_specs = P(("row", "col"), None, None, None)
    return jax.shard_map(shards, mesh=mesh, in_specs=in_specs, out_specs=out_specs, check_vma=False)
```
